256 devices in a mesh: pair: 8 (over x, core), node: 32 (over z, y).
Axes of the slice: x: 4, y: 4, z: 8, core: 2. Of those that a mesh axis runs over, the one named last changes fastest.
Arguments:
- features: bfloat16 [32768, 256], P('node', 'pair'), may hold values from -60 to 60
- neighbors: int32 [8, 32768, 10], P('pair', 'node'), may hold values from 0 to 32767, as said below
- counts: int32 [8, 32768], P('pair', 'node'), may hold values from 1 to 10
- pairs: int32 [1048576, 2], P(('pair', 'node')), may hold values from 0 to 32767, as said below
- w_self: bfloat16 [256, 256], replicated, may hold values from -0.25 to 0.25
- w_neigh: bfloat16 [256, 256], replicated, may hold values from -0.25 to 0.25
- b_layer: float32 [256], replicated, may hold values from -3 to 3
- w_one: bfloat16 [256, 256], replicated, may hold values from -0.375 to 0.375
- b_one: float32 [256], replicated, may hold values from -3 to 3
- w_two: bfloat16 [256, 256], replicated, may hold values from -0.375 to 0.375
- b_two: float32 [256], replicated, may hold values from -3 to 3
- w_out: float32 [256], replicated, may hold values from -0.375 to 0.375
Outputs:
- pair_loss: float32 [1048576], P(('pair', 'node'))
The draws below stay inside these ranges and needn't reach their ends.
Inputs may be any that keep to these rules, and one draw needn't show every extreme that they name: `neighbors`: within one list block (one micro-batch, the 1024 nodes of one node range) at most 640 slots name nodes of any one node range; in every micro-batch one node range receives exactly 640 from every block. `pairs`: within the 4096 rows of one device at most 512 endpoints lie in any one node range; in every micro-batch one node range receives exactly 512 from every device.
All inputs are finite; a program needn't handle non-finite values.
Results may differ from the reference program's by a relative error of at most 0.0032.
Values may be sent and summed in bfloat16 or wider, within the bound.
No kernel may reach another device: no remote copies, remote signals or barrier semaphores. Data moves between devices by JAX's collectives and lax.ppermute only.
A program may use at most 128 MiB of HBM per device.

```python
import math
import jax
import jax.numpy as jnp
from jax import lax

D = 256
FANOUT = 10
NODE_DEV = 1024
PAIR_DEV = 4096
GROUPS = 8
SHARDS = 32
NODES = 32768
PAIRS = 1048576


def owned_ids(key, hot, slots, shards, per_shard):
    mean_load = slots // shards
    half = shards // 2
    perm = jax.random.permutation(jax.random.fold_in(key, 11), shards).astype(jnp.int32)
    place = jnp.arange(shards, dtype=jnp.int32)
    first = perm[0]
    perm = jnp.where(perm == hot, first, perm)
    perm = jnp.where(place == 0, hot, perm)
    spread = jax.random.randint(jax.random.fold_in(key, 12), (half,), 0, mean_load + 1).astype(jnp.int32)
    spread = jnp.where(jnp.arange(half, dtype=jnp.int32) == 0, mean_load, spread)
    loads = jnp.zeros((shards,), jnp.int32)
    loads = loads.at[perm[0::2]].set(mean_load + spread)
    loads = loads.at[perm[1::2]].set(mean_load - spread)
    ends = jnp.cumsum(loads).astype(jnp.int32)
    position = jnp.arange(slots, dtype=jnp.int32)
    owner = jnp.sum((ends[None, :] <= position[:, None]).astype(jnp.int32), axis=1)
    order = jax.random.permutation(jax.random.fold_in(key, 13), slots).astype(jnp.int32)
    owner = owner[order]
    offset = jax.random.randint(jax.random.fold_in(key, 14), (slots,), 0, per_shard).astype(jnp.int32)
    return owner * per_shard + offset


def group_hots(key, count):
    return jax.random.randint(jax.random.fold_in(key, 21), (count,), 0, SHARDS).astype(jnp.int32)


def draw_neighbors(key, part):
    key = jax.random.fold_in(key, 1)
    hots = group_hots(key, GROUPS)
    blocks = jnp.arange(GROUPS * SHARDS, dtype=jnp.int32)

    def one_block(block):
        return owned_ids(jax.random.fold_in(key, block), hots[block // SHARDS], NODE_DEV * FANOUT, SHARDS, NODE_DEV)
    ids = jax.vmap(one_block)(blocks)
    return ids.reshape(GROUPS, NODES, FANOUT)


def draw_pairs(key, part):
    key = jax.random.fold_in(key, 2)
    hots = group_hots(key, GROUPS)
    blocks = jnp.arange(GROUPS * SHARDS, dtype=jnp.int32)

    def one_block(block):
        return owned_ids(jax.random.fold_in(key, block), hots[block // SHARDS], 2 * PAIR_DEV, SHARDS, NODE_DEV)
    ids = jax.vmap(one_block)(blocks)
    return ids.reshape(PAIRS, 2)


def draw_features(key, part):
    key = jax.random.fold_in(key, 3)
    scales = jnp.exp(jax.random.uniform(jax.random.fold_in(key, 31), (NODES, 1), jnp.float32, 0.0, math.log(10.0)))
    base = jnp.clip(jax.random.normal(jax.random.fold_in(key, 32), (NODES, D), jnp.float32), -6.0, 6.0)
    values = base * scales
    return values.astype(jnp.bfloat16)


def place_ends(entries, stream_key, least, largest):
    longest = entries.shape.index(max(entries.shape))
    spots = []
    for shift in (0, 1):
        where = [jax.random.randint(jax.random.fold_in(stream_key, axis), (), 0, length) for axis, length in enumerate(entries.shape)]
        where[longest] = (where[longest] + shift) % entries.shape[longest]
        spots.append(tuple(where))
    return entries.at[spots[0]].set(least).at[spots[1]].set(largest)


def scatter_about(rng, extent, deviation, most, held_as=jnp.bfloat16):
    entries = deviation * jax.random.normal(rng, extent, jnp.float32)
    return jnp.clip(entries, min=-most, max=most).astype(held_as)


def setup_inputs(seed: int = 0) -> dict:
    arg_keys = jax.random.split(jax.random.key(seed), 13)
    features = draw_features(jax.random.fold_in(arg_keys[12], 71), 0)
    neighbors = draw_neighbors(jax.random.fold_in(arg_keys[12], 71), 0)
    counts = place_ends(jax.random.randint(arg_keys[2], (GROUPS, NODES), 1, FANOUT + 1), jax.random.fold_in(arg_keys[2], 1), 1, FANOUT).astype(jnp.int32)
    pairs = draw_pairs(jax.random.fold_in(arg_keys[12], 71), 0)
    w_self = scatter_about(arg_keys[4], (D, D), (2 * D) ** -0.5, 0.25)
    w_neigh = scatter_about(arg_keys[5], (D, D), (2 * D) ** -0.5, 0.25)
    b_layer = scatter_about(arg_keys[6], (D,), 0.5, 3.0, jnp.float32)
    w_one = scatter_about(arg_keys[7], (D, D), D ** -0.5, 0.375)
    b_one = scatter_about(arg_keys[8], (D,), 0.5, 3.0, jnp.float32)
    w_two = scatter_about(arg_keys[9], (D, D), D ** -0.5, 0.375)
    b_two = scatter_about(arg_keys[10], (D,), 0.5, 3.0, jnp.float32)
    w_out = scatter_about(arg_keys[11], (D,), D ** -0.5, 0.375, jnp.float32)
    return dict(features=features, neighbors=neighbors, counts=counts, pairs=pairs, w_self=w_self, w_neigh=w_neigh, b_layer=b_layer, w_one=w_one, b_one=b_one, w_two=w_two, b_two=b_two, w_out=w_out)


def reference(features, neighbors, counts, pairs, w_self, w_neigh, b_layer, w_one, b_one, w_two, b_two, w_out):
    self_term = jnp.dot(features, w_self, preferred_element_type=jnp.float32)
    pair_groups = pairs.reshape(GROUPS, PAIRS // GROUPS, 2)
    slot_index = jnp.arange(FANOUT, dtype=jnp.int32)

    def one_group(inputs):
        nbr, cnt, ends = inputs
        valid = slot_index[None, :] < cnt[:, None]
        rows = jnp.take(features, nbr, axis=0).astype(jnp.float32)
        summed = lax.optimization_barrier(jnp.sum(jnp.where(valid[:, :, None], rows, jnp.float32(0.0)), axis=1))
        mean_nbr = (summed / cnt[:, None].astype(jnp.float32)).astype(jnp.bfloat16)
        pre = self_term + jnp.dot(mean_nbr, w_neigh, preferred_element_type=jnp.float32) + b_layer
        act = jnp.maximum(pre, 0.0)
        embed = (act * lax.rsqrt(lax.optimization_barrier(jnp.mean(act * act, axis=-1, keepdims=True)) + 1e-06)).astype(jnp.bfloat16)
        left = jnp.take(embed, ends[:, 0], axis=0).astype(jnp.float32)
        right = jnp.take(embed, ends[:, 1], axis=0).astype(jnp.float32)
        hadamard = (left * right).astype(jnp.bfloat16)
        first = jnp.maximum(jnp.dot(hadamard, w_one, preferred_element_type=jnp.float32) + b_one, 0.0).astype(jnp.bfloat16)
        second = jnp.maximum(jnp.dot(first, w_two, preferred_element_type=jnp.float32) + b_two, 0.0)
        logit = jnp.dot(second, w_out, precision=lax.Precision.HIGHEST)
        return logit
    logits = lax.map(one_group, (neighbors, counts, pair_groups)).reshape(PAIRS)
    positive = jnp.arange(PAIRS, dtype=jnp.int32) % PAIR_DEV < PAIR_DEV // 4
    return jnp.where(positive, jax.nn.softplus(-logits), jax.nn.softplus(logits))
```

```python
import functools
import jax
import jax.numpy as jnp
from jax import lax
from jax.experimental import pallas as pl
from jax.experimental.pallas import tpu as pltpu
from jax.sharding import PartitionSpec as P

def gather_kernel(starts, keys, words, tab_hbm, wcat, bl, w1, b1, w2, b2, wo, out, tab, sums, selfs, sem, *, npair, span, U):
    cp = pltpu.make_async_copy(tab_hbm, tab, sem)
    cp.start(); cp.wait()
    mask16 = 65535

    def one(i, c):
        key = keys[i]
        e2 = (key & 8191) * 2
        n = lax.shift_right_logical(key, 13) & 32767
        base = n + lax.shift_right_logical(n, 10) * (4 * span)
        acc = None
        for j in range((c + 1) // 2):
            w = words[base + j * span]
            r = tab[w & mask16].astype(jnp.float32)
            acc = r if acc is None else acc + r
            if 2 * j + 1 < c:
                r = tab[lax.shift_right_logical(w, 16)].astype(jnp.float32)
                acc = acc + r
        if c > 1:
            acc = acc * jnp.float32(1.0 / c)
        return e2, n, acc

    def put(e2, n, acc):
        sums[pl.ds(e2, 2), :] = acc
        selfs[pl.ds(e2, 2), :] = tab[n].astype(jnp.float32)

    for c in range(1, 11):
        lo = starts[c - 1]
        hi = starts[c]
        nb = lax.div(hi - lo, U)
        def body(t, carry, c=c, lo=lo):
            res = [one(lo + t * U + u, c) for u in range(U)]
            for r in res: put(*r)
            return carry
        lax.fori_loop(0, nb, body, 0)
        def rem(t, carry, c=c):
            put(*one(t, c))
            return carry
        lax.fori_loop(lo + nb * U, hi, rem, 0)

    B = 512
    def dense(t, carry):
        embs = []
        for s in range(2):
            r0 = (s * npair + t * B) * 2
            xs = []
            for ref in (selfs, sums):
                for h in range(2):
                    xs.append(ref[pl.ds(r0 + h, B, 2), :].astype(jnp.bfloat16))
            x = jnp.concatenate(xs, axis=1)
            pre = jnp.dot(x, wcat[...], preferred_element_type=jnp.float32) + bl[...]
            r = jnp.maximum(pre, 0.0)
            ms = jnp.mean(r * r, axis=-1, keepdims=True)
            embs.append((r * lax.rsqrt(ms + 1e-6)).astype(jnp.bfloat16).astype(jnp.float32))
        had = (embs[0] * embs[1]).astype(jnp.bfloat16)
        first = jnp.maximum(jnp.dot(had, w1[...], preferred_element_type=jnp.float32) + b1[...], 0.0).astype(jnp.bfloat16)
        second = jnp.maximum(jnp.dot(first, w2[...], preferred_element_type=jnp.float32) + b2[...], 0.0)
        prod = second * wo[...]
        part = prod[:, :128] + prod[:, 128:]
        logit = lax.dot_general(jnp.ones((8, 128), jnp.float32), part, (((1,), (1,)), ((), ())), precision=lax.Precision.HIGHEST, preferred_element_type=jnp.float32)[:1]
        k = t * B + lax.broadcasted_iota(jnp.int32, (1, B), 1)
        z = jnp.where(k < npair // 4, -logit, logit)
        out[pl.ds(t, 1), :] = jnp.maximum(z, 0.0) + jnp.log1p(jnp.exp(-jnp.abs(z)))
        return carry
    lax.fori_loop(0, npair // B, dense, 0)

def score(starts, keys, words, table, wcat, bl, w1, b1, w2, b2, wo, U=5, npair=4096, span=1024):
    nodes = table.shape[0]
    smem = pl.BlockSpec(memory_space=pltpu.SMEM)
    vm = pl.BlockSpec(memory_space=pltpu.VMEM)
    return pl.pallas_call(
        functools.partial(gather_kernel, npair=npair, span=span, U=U),
        out_shape=jax.ShapeDtypeStruct((npair // 512, 512), jnp.float32),
        in_specs=[smem, smem, smem, pl.BlockSpec(memory_space=pl.ANY)] + [vm] * 7,
        out_specs=vm,
        scratch_shapes=[pltpu.VMEM((nodes, 2, 128), jnp.bfloat16), pltpu.VMEM((4 * npair, 128), jnp.float32), pltpu.VMEM((4 * npair, 128), jnp.float32), pltpu.SemaphoreType.DMA],
        compiler_params=pltpu.CompilerParams(vmem_limit_bytes=56 * 2**20),
    )(starts, keys, words, table, wcat, bl, w1, b1, w2, b2, wo)


def on_device(
    features, neighbors, counts, pairs, w_self, w_neigh, b_layer, w_one, b_one, w_two, b_two, w_out
):
    span, cols = features.shape
    shards = lax.axis_size("node")
    parts = lax.axis_size("pair")
    npair = pairs.shape[0]
    slab = lax.all_to_all(
        features.reshape(parts, span // parts, cols), "pair", split_axis=0, concat_axis=0, tiled=True
    )
    slab = slab.transpose(1, 0, 2).reshape(span // parts, 2, parts * cols // 2)
    table = lax.all_gather(slab, ("node", "pair"), axis=0, tiled=True)
    ids = neighbors[0].T
    words = ids[0::2] | (ids[1::2] << 16)
    info = lax.all_gather(jnp.concatenate([words, counts], axis=0), "node", axis=0)
    words = info[:, :5].reshape(-1)
    ends = pairs.T.reshape(-1)
    cnt = jnp.take(info[:, 5].reshape(-1), ends, axis=0)
    key = ((cnt - 6) << 28) | (ends << 13) | jnp.arange(2 * npair, dtype=jnp.int32)
    key = lax.sort(key)
    starts = jnp.sum(
        (cnt[None, :] <= jnp.arange(11, dtype=jnp.int32)[:, None]).astype(jnp.int32), axis=1
    )
    row = lambda v: v.reshape(1, -1)
    loss = score(
        starts, key, words, table, jnp.concatenate([w_self, w_neigh], axis=0), row(b_layer),
        w_one, row(b_one), w_two, row(b_two), row(w_out), npair=npair, span=span,
    )
    return loss.reshape(-1)


def solution(mesh):
    in_specs = (
        P("node", "pair"),
        P("pair", "node", None),
        P("pair", "node"),
        P(("pair", "node"), None),
    ) + (P(),) * 8
    return jax.shard_map(
        on_device, mesh=mesh, in_specs=in_specs, out_specs=P(("pair", "node")), check_vma=False
    )
```

```python
import functools
import jax
import jax.numpy as jnp
from jax import lax
from jax.experimental import pallas as pl
from jax.experimental.pallas import tpu as pltpu
from jax.sharding import Mesh
from jax.sharding import PartitionSpec as P

NY, NZ, NCORE = 4, 8, 2
QUARTERS = 4
FAN = 10
STEP = 16
STEPS = (16, 12, 10, 8, 6, 3, 2, 2, 2, 2)
SMEM = pl.BlockSpec(memory_space=pltpu.SMEM)
VMEM = pl.BlockSpec(memory_space=pltpu.VMEM)
ANY = pl.BlockSpec(memory_space=pl.ANY)


def look_up_kernel(where, values, out, *, step):
    def body(t, carry):
        for u in range(step):
            out[t * step + u] = values[where[t * step + u]]
        return carry

    lax.fori_loop(0, where.shape[0] // step, body, 0)


def look_up(where, values):
    return pl.pallas_call(
        functools.partial(look_up_kernel, step=STEP),
        out_shape=jax.ShapeDtypeStruct(where.shape, jnp.int32),
        in_specs=[SMEM] * 2,
        out_specs=SMEM,
        cost_estimate=pl.CostEstimate(flops=0, bytes_accessed=2**25, transcendentals=0),
    )(where, values)


def score_kernel(*refs, npair):
    starts, e2s, spots, owns, ids_hbm = refs[:5]
    table, mats, vecs, out, tab, sums, selfs, tab_sem, ids_sem = refs[5:14]
    ids = refs[14:]
    part = ids_hbm.shape[0] // (QUARTERS * FAN)

    def fetch(q):
        slot = q & 1
        return [
            pltpu.make_async_copy(
                ids_hbm.at[pl.ds((q * FAN + j) * part, part)],
                ids[j].at[pl.ds(slot * part, part)],
                ids_sem.at[slot, j],
            )
            for j in range(FAN)
        ]

    for copy in fetch(0):
        copy.start()
    pltpu.make_async_copy(table, tab, tab_sem).start()
    pltpu.make_async_copy(table, tab, tab_sem).wait()

    def load(n):
        return tab[n].astype(jnp.float32)

    def one(i, c):
        spot = spots[i]
        rows = [load(ids[j][spot]) for j in range(c)]
        while len(rows) > 1:
            rows = [sum(rows[k + 1 : k + 2], rows[k]) for k in range(0, len(rows), 2)]
        acc = rows[0]
        if c > 1:
            acc = acc * jnp.float32(1.0 / c)
        return pl.multiple_of(e2s[i], 2), acc, load(owns[i])

    def put(e2, acc, own):
        sums[pl.ds(e2, 2), :] = acc
        selfs[pl.ds(e2, 2), :] = own

    def quarter(q, carry):
        for copy in fetch(q):
            copy.wait()

        @pl.when(q < QUARTERS - 1)
        def _():
            for copy in fetch(q + 1):
                copy.start()

        for c in range(1, FAN + 1):
            lo = starts[q * FAN + c - 1]
            hi = starts[q * FAN + c]
            step = STEPS[c - 1]

            def body(i, c=c, step=step):
                for r in [one(i + u, c) for u in range(step)]:
                    put(*r)
                return i + step

            def rest(i, c=c):
                put(*one(i, c))
                return i + 1

            lo = lax.while_loop(lambda i: i <= hi - step, body, lo)
            lax.while_loop(lambda i: i < hi, rest, lo)
        return carry

    lax.fori_loop(0, QUARTERS, quarter, 0)

    rows = 512

    def dense(t, carry):
        embs = []
        for side in range(2):
            r0 = (side * npair + t * rows) * 2
            x = jnp.concatenate(
                [
                    ref[pl.ds(r0 + h, rows, 2), :].astype(jnp.bfloat16)
                    for ref in (selfs, sums)
                    for h in range(2)
                ],
                axis=1,
            )
            pre = jnp.dot(x, mats[:512], preferred_element_type=jnp.float32) + vecs[0:1]
            act = jnp.maximum(pre, 0.0)
            ms = jnp.mean(act * act, axis=-1, keepdims=True)
            embs.append((act * lax.rsqrt(ms + 1e-6)).astype(jnp.bfloat16).astype(jnp.float32))
        had = (embs[0] * embs[1]).astype(jnp.bfloat16)
        first = jnp.dot(had, mats[512:768], preferred_element_type=jnp.float32) + vecs[1:2]
        first = jnp.maximum(first, 0.0).astype(jnp.bfloat16)
        second = jnp.dot(first, mats[768:], preferred_element_type=jnp.float32) + vecs[2:3]
        second = jnp.maximum(second, 0.0) * vecs[3:4]
        logit = lax.dot_general(
            jnp.ones((8, 128), jnp.float32),
            second[:, :128] + second[:, 128:],
            (((1,), (1,)), ((), ())),
            precision=lax.Precision.HIGHEST,
            preferred_element_type=jnp.float32,
        )[:1]
        k = t * rows + lax.broadcasted_iota(jnp.int32, (1, rows), 1)
        x = jnp.where(k < npair // 4, -logit, logit)
        out[pl.ds(t, 1), :] = jnp.maximum(x, 0.0) + jnp.log1p(jnp.exp(-jnp.abs(x)))
        return carry

    lax.fori_loop(0, npair // rows, dense, 0)


def score(starts, e2s, spots, owns, ids, table, mats, vecs, npair):
    nodes = table.shape[0]
    return pl.pallas_call(
        functools.partial(score_kernel, npair=npair),
        out_shape=jax.ShapeDtypeStruct((npair // 512, 512), jnp.float32),
        in_specs=[SMEM] * 4 + [ANY] * 2 + [VMEM] * 2,
        out_specs=VMEM,
        scratch_shapes=[
            pltpu.VMEM((nodes, 2, 128), jnp.bfloat16),
            pltpu.VMEM((4 * npair, 128), jnp.float32),
            pltpu.VMEM((4 * npair, 128), jnp.float32),
            pltpu.SemaphoreType.DMA,
            pltpu.SemaphoreType.DMA((2, FAN)),
        ]
        + [pltpu.SMEM((2 * ids.shape[0] // (QUARTERS * FAN),), jnp.int32)] * FAN,
        compiler_params=pltpu.CompilerParams(vmem_limit_bytes=56 * 2**20),
    )(starts, e2s, spots, owns, ids, table, mats, vecs)


def shift(x, axis, by):
    n = lax.axis_size(axis)
    return lax.ppermute(x, axis, [(i, (i + by) % n) for i in range(n)])


def around(x, axis, split):
    n = lax.axis_size(axis)
    low, high = [shift(x, axis, 1)], [shift(x, axis, -1)]
    for _ in range(n // 2 - 2):
        low.append(shift(low[-1], axis, 1))
        high.append(shift(high[-1], axis, -1))
    far = [shift(low[-1][:split], axis, 1), shift(high[-1][split:], axis, -1)]
    return [x] + high + far + low[::-1]


def spread(mine, half):
    a, b = mine[: 2 * half], mine[2 * half :]
    row = jnp.concatenate(around(a, "z", half))
    col = jnp.concatenate(around(b, "y", half))
    return around(row, "y", row.shape[0] // 2) + around(col, "z", col.shape[0] // 2)


def moved(ids, z, y, core, half):
    block = 2 * half
    dz = ((ids // (4 * block * NY)) - z) & (NZ - 1)
    dy = ((ids // (4 * block)) - y) & (NY - 1)
    other = (ids // (2 * block) & 1) ^ core
    lane = ids // block & 1
    slot = jnp.where(lane == 0, dy * NZ + dz, dz * NY + dy)
    return ((other * 2 + lane) * (NZ * NY) + slot) * block + (ids & (block - 1))


def on_device(
    features, neighbors, counts, pairs, w_self, w_neigh, b_layer, w_one, b_one, w_two, b_two, w_out
):
    span = features.shape[0]
    nodes = span * NZ * NY
    npair = pairs.shape[0]
    half = span // 8
    z, y, core = (lax.axis_index(a) for a in ("z", "y", "core"))
    info = jnp.concatenate([neighbors[0].T.reshape(-1), counts[0]]).astype(jnp.int16)
    split = info.shape[0] // 2
    info = jnp.concatenate(around(info, "y", split))
    info = jnp.concatenate(around(info, "z", 2 * info.shape[0] // 4))
    info = info.reshape(NZ * NY, -1)
    cnt = info[:, FAN * span :].astype(jnp.int32).reshape(-1)
    table = lax.all_gather(features, ("x", "core"), axis=1, tiled=True).reshape(span, 2, 128)
    mine = lax.dynamic_slice_in_dim(table, core * (4 * half), 4 * half, 0)
    mine = spread(mine, half)
    table = jnp.concatenate(mine + [shift(part, "core", 1) for part in mine])
    ends = pairs.T.reshape(-1)
    near = (((ends // (span * NY) - z) & (NZ - 1)) * NY + ((ends // span - y) & (NY - 1))) * span
    near = near + (ends & (span - 1))
    share = nodes // QUARTERS
    code = near // share * FAN + look_up(near, cnt) - 1
    keys = ((code - 32) << 26) | ((near & (share - 1)) << 13) | jnp.arange(2 * npair, dtype=jnp.int32)
    keys = lax.sort(keys)
    marks = jnp.arange(QUARTERS * FAN + 1, dtype=jnp.int32)
    starts = jnp.sum((code[None, :] < marks[:, None]).astype(jnp.int32), axis=1)
    e2s = (keys & 8191) * 2
    part = ((keys >> 26) + 32) // FAN
    near = (keys >> 13) & (share - 1)
    spots = near + (part & 1) * share
    near = near + part * share
    own = ((near // (span * NY) + z) & (NZ - 1)) * NY + ((near // span + y) & (NY - 1))
    owns = moved(own * span + (near & (span - 1)), z, y, core, half)
    ids = info[:, : FAN * span].astype(jnp.int32).reshape(QUARTERS, -1, FAN, span)
    ids = moved(ids.transpose(0, 2, 1, 3).reshape(-1), z, y, core, half)
    mats = jnp.concatenate([w_self, w_neigh, w_one, w_two], axis=0)
    vecs = jnp.stack([b_layer, b_one, b_two, w_out])
    loss = score(starts, e2s, spots, owns, ids, table, mats, vecs, npair)
    return loss.reshape(-1)


def solution(mesh):
    axes = ("x", "core", "z", "y")
    grid = Mesh(mesh.devices.reshape(-1, NCORE, NZ, NY), axes)
    in_specs = (
        P(("z", "y"), ("x", "core")),
        P(("x", "core"), ("z", "y"), None),
        P(("x", "core"), ("z", "y")),
        P(axes, None),
    ) + (P(),) * 8
    return jax.shard_map(
        on_device, mesh=grid, in_specs=in_specs, out_specs=P(axes), check_vma=False
    )
```

```python
import functools
import jax
import jax.numpy as jnp
from jax import lax
from jax.experimental import pallas as pl
from jax.experimental.pallas import tpu as pltpu
from jax.sharding import PartitionSpec as P

QUARTERS = 4
FAN = 10
WORDS = FAN // 2
STEP = 16
MOVES = 32
STEPS = (8, 8, 8, 8, 8, 8, 8, 8, 8, 8)
SMEM = pl.BlockSpec(memory_space=pltpu.SMEM)
VMEM = pl.BlockSpec(memory_space=pltpu.VMEM)
ANY = pl.BlockSpec(memory_space=pl.ANY)


def look_up_kernel(where, values, out, *, step):
    def body(t, carry):
        for u in range(step):
            out[t * step + u] = values[where[t * step + u]]
        return carry

    lax.fori_loop(0, where.shape[0] // step, body, 0)


def look_up(where, values):
    return pl.pallas_call(
        functools.partial(look_up_kernel, step=STEP),
        out_shape=jax.ShapeDtypeStruct(where.shape, jnp.int32),
        in_specs=[SMEM] * 2,
        out_specs=SMEM,
        cost_estimate=pl.CostEstimate(flops=0, bytes_accessed=2**25, transcendentals=0),
    )(where, values)


def score_kernel(*refs, npair):
    starts, spots, moves, ids_hbm = refs[:4]
    table, mats, vecs, out, tab, means, sums, selfs, tab_sem, ids_sem = refs[4:14]
    ids = refs[14:]
    part = ids_hbm.shape[0] // (QUARTERS * WORDS)

    def fetch(q):
        slot = q & 1
        return [
            pltpu.make_async_copy(
                ids_hbm.at[pl.ds((q * WORDS + j) * part, part)],
                ids[j].at[pl.ds(slot * part, part)],
                ids_sem.at[slot, j],
            )
            for j in range(WORDS)
        ]

    for copy in fetch(0):
        copy.start()
    pltpu.make_async_copy(table, tab, tab_sem).start()
    pltpu.make_async_copy(table, tab, tab_sem).wait()

    def load(n):
        return tab[n].astype(jnp.float32)

    def one(i, c):
        spot = spots[i]
        words = [ids[j][spot] for j in range((c + 1) // 2)]
        rows = [
            load(lax.shift_right_logical(words[j // 2], 16) if j % 2 else words[j // 2] & 65535)
            for j in range(c)
        ]
        while len(rows) > 1:
            rows = [sum(rows[k + 1 : k + 2], rows[k]) for k in range(0, len(rows), 2)]
        return rows[0] if c == 1 else rows[0] * jnp.float32(1.0 / c)

    def quarter(q, carry):
        for copy in fetch(q):
            copy.wait()

        @pl.when(q < QUARTERS - 1)
        def _():
            for copy in fetch(q + 1):
                copy.start()

        for c in range(1, FAN + 1):
            lo = starts[q * FAN + c - 1]
            hi = starts[q * FAN + c]
            step = STEPS[c - 1]

            def body(i, c=c, step=step):
                got = [one(i + u, c) for u in range(step)]
                for u in range(step):
                    means[pl.ds(2 * i + 2 * u, 2), :] = got[u]
                return i + step

            def rest(i, c=c):
                means[pl.ds(2 * i, 2), :] = one(i, c)
                return i + 1

            lo = lax.while_loop(lambda i: i <= hi - step, body, lo)
            lax.while_loop(lambda i: i < hi, rest, lo)
        return carry

    lax.fori_loop(0, QUARTERS, quarter, 0)

    def own(t, carry):
        i = t * MOVES
        move = [moves[i + u] for u in range(MOVES)]
        got = [load(move[u] & 65535) for u in range(MOVES)]
        for u in range(MOVES):
            selfs[pl.ds(2 * i + 2 * u, 2), :] = got[u]
        got = [means[pl.ds(2 * i + 2 * u, 2), :] for u in range(MOVES)]
        for u in range(MOVES):
            e2 = pl.multiple_of(lax.shift_right_logical(move[u], 16), 2)
            sums[pl.ds(e2, 2), :] = got[u]
        return carry

    lax.fori_loop(0, 2 * npair // MOVES, own, 0)

    rows = 512

    def dense(t, carry):
        embs = []
        for side in range(2):
            r0 = (side * npair + t * rows) * 2
            x = jnp.concatenate(
                [
                    ref[pl.ds(r0 + h, rows, 2), :].astype(jnp.bfloat16)
                    for ref in (selfs, sums)
                    for h in range(2)
                ],
                axis=1,
            )
            pre = jnp.dot(x, mats[:512], preferred_element_type=jnp.float32) + vecs[0:1]
            act = jnp.maximum(pre, 0.0)
            ms = jnp.mean(act * act, axis=-1, keepdims=True)
            embs.append((act * lax.rsqrt(ms + 1e-6)).astype(jnp.bfloat16).astype(jnp.float32))
        had = (embs[0] * embs[1]).astype(jnp.bfloat16)
        first = jnp.dot(had, mats[512:768], preferred_element_type=jnp.float32) + vecs[1:2]
        first = jnp.maximum(first, 0.0).astype(jnp.bfloat16)
        second = jnp.dot(first, mats[768:], preferred_element_type=jnp.float32) + vecs[2:3]
        second = jnp.maximum(second, 0.0) * vecs[3:4]
        logit = lax.dot_general(
            jnp.ones((8, 128), jnp.float32),
            second[:, :128] + second[:, 128:],
            (((1,), (1,)), ((), ())),
            precision=lax.Precision.HIGHEST,
            preferred_element_type=jnp.float32,
        )[:1]
        k = t * rows + lax.broadcasted_iota(jnp.int32, (1, rows), 1)
        x = jnp.where(k < npair // 4, -logit, logit)
        out[pl.ds(t, 1), :] = jnp.maximum(x, 0.0) + jnp.log1p(jnp.exp(-jnp.abs(x)))
        return carry

    lax.fori_loop(0, npair // rows, dense, 0)


def score(starts, spots, moves, ids, table, mats, vecs, npair):
    nodes = table.shape[0]
    return pl.pallas_call(
        functools.partial(score_kernel, npair=npair),
        out_shape=jax.ShapeDtypeStruct((npair // 512, 512), jnp.float32),
        in_specs=[SMEM] * 3 + [ANY] * 2 + [VMEM] * 2,
        out_specs=VMEM,
        scratch_shapes=[
            pltpu.VMEM((nodes, 2, 128), jnp.bfloat16),
            pltpu.VMEM((4 * npair, 128), jnp.float32),
            pltpu.VMEM((4 * npair, 128), jnp.float32),
            pltpu.VMEM((4 * npair, 128), jnp.float32),
            pltpu.SemaphoreType.DMA,
            pltpu.SemaphoreType.DMA((2, WORDS)),
        ]
        + [pltpu.SMEM((2 * ids.shape[0] // (QUARTERS * WORDS),), jnp.int32)] * WORDS,
        compiler_params=pltpu.CompilerParams(vmem_limit_bytes=56 * 2**20),
    )(starts, spots, moves, ids, table, mats, vecs)


def on_device(
    features, neighbors, counts, pairs, w_self, w_neigh, b_layer, w_one, b_one, w_two, b_two, w_out
):
    span, cols = features.shape
    parts, shards = lax.axis_size("pair"), lax.axis_size("node")
    npair = pairs.shape[0]
    slab = lax.all_to_all(
        features.reshape(parts, span // parts, cols), "pair", split_axis=0, concat_axis=0, tiled=True
    )
    slab = slab.transpose(1, 0, 2).reshape(span // parts, 2, parts * cols // 2)
    table = lax.all_gather(slab, ("node", "pair"), axis=0, tiled=True)
    ids = neighbors[0].T
    info = jnp.concatenate([ids[0::2] | (ids[1::2] << 16), counts], axis=0)
    info = lax.all_gather(info, "node", axis=0)
    share = span * shards // QUARTERS
    ids = info[:, :WORDS].reshape(QUARTERS, -1, WORDS, span).transpose(0, 2, 1, 3).reshape(-1)
    ends = pairs.T.reshape(-1)
    code = ends // share * FAN + look_up(ends, info[:, WORDS].reshape(-1)) - 1
    keys = ((code - 32) << 26) | ((ends & (share - 1)) << 13) | jnp.arange(2 * npair, dtype=jnp.int32)
    keys = lax.sort(keys)
    marks = jnp.arange(QUARTERS * FAN + 1, dtype=jnp.int32)
    starts = jnp.sum((code[None, :] < marks[:, None]).astype(jnp.int32), axis=1)
    moves = ends | ((keys & 8191) << 17)
    spots = ((keys >> 13) & (share - 1)) + (((keys >> 26) + 32) // FAN & 1) * share
    mats = jnp.concatenate([w_self, w_neigh, w_one, w_two], axis=0)
    vecs = jnp.stack([b_layer, b_one, b_two, w_out])
    loss = score(starts, spots, moves, ids, table, mats, vecs, npair)
    return loss.reshape(-1)


def solution(mesh):
    in_specs = (
        P("node", "pair"),
        P("pair", "node", None),
        P("pair", "node"),
        P(("pair", "node"), None),
    ) + (P(),) * 8
    return jax.shard_map(
        on_device, mesh=mesh, in_specs=in_specs, out_specs=P(("pair", "node")), check_vma=False
    )
```

```python
import functools
import jax
import jax.numpy as jnp
from jax import lax
from jax.experimental import pallas as pl
from jax.experimental.pallas import tpu as pltpu
from jax.sharding import PartitionSpec as P

QUARTERS = 4
FAN = 10
WORDS = FAN // 2
STEP = 16
MOVES = 32
ROWS = 1024
STEPS = (12, 12, 12, 12, 12, 12, 12, 12, 12, 12)
SMEM = pl.BlockSpec(memory_space=pltpu.SMEM)
VMEM = pl.BlockSpec(memory_space=pltpu.VMEM)
ANY = pl.BlockSpec(memory_space=pl.ANY)


def look_up_kernel(where, values, out, *, step):
    def body(t, carry):
        for u in range(step):
            out[t * step + u] = values[where[t * step + u]]
        return carry

    lax.fori_loop(0, where.shape[0] // step, body, 0)


def look_up(where, values):
    return pl.pallas_call(
        functools.partial(look_up_kernel, step=STEP),
        out_shape=jax.ShapeDtypeStruct(where.shape, jnp.int32),
        in_specs=[SMEM] * 2,
        out_specs=SMEM,
        cost_estimate=pl.CostEstimate(flops=0, bytes_accessed=2**25, transcendentals=0),
    )(where, values)


def score_kernel(*refs, npair):
    starts, spots_hbm, moves_hbm, ids_hbm = refs[:4]
    table, mats, vecs, out, tab, means, sums, selfs, tab_sem, ids_sem, list_sem, spots, moves = refs[4:17]
    ids = refs[17:]
    part = ids_hbm.shape[0] // (QUARTERS * WORDS)

    def fetch(q):
        slot = q & 1
        return [
            pltpu.make_async_copy(
                ids_hbm.at[pl.ds((q * WORDS + j) * part, part)],
                ids[j].at[pl.ds(slot * part, part)],
                ids_sem.at[slot, j],
            )
            for j in range(WORDS)
        ]

    for copy in fetch(0):
        copy.start()
    lists = [
        pltpu.make_async_copy(spots_hbm, spots, list_sem.at[0]),
        pltpu.make_async_copy(moves_hbm, moves, list_sem.at[1]),
    ]
    for copy in lists:
        copy.start()
    pltpu.make_async_copy(table, tab, tab_sem).start()
    pltpu.make_async_copy(table, tab, tab_sem).wait()
    for copy in lists:
        copy.wait()

    def load(n):
        return tab[n].astype(jnp.float32)

    def one(i, c):
        spot = spots[i]
        words = [ids[j][spot] for j in range((c + 1) // 2)]
        rows = [
            load(lax.shift_right_logical(words[j // 2], 16) if j % 2 else words[j // 2] & 65535)
            for j in range(c)
        ]
        while len(rows) > 1:
            rows = [sum(rows[k + 1 : k + 2], rows[k]) for k in range(0, len(rows), 2)]
        return rows[0] if c == 1 else rows[0] * jnp.float32(1.0 / c)

    def quarter(q, carry):
        for copy in fetch(q):
            copy.wait()

        @pl.when(q < QUARTERS - 1)
        def _():
            for copy in fetch(q + 1):
                copy.start()

        for c in range(1, FAN + 1):
            lo = starts[q * FAN + c - 1]
            hi = starts[q * FAN + c]
            step = STEPS[c - 1]

            def body(i, c=c, step=step):
                got = [one(i + u, c) for u in range(step)]
                for u in range(step):
                    means[pl.ds(2 * i + 2 * u, 2), :] = got[u]
                return i + step

            def rest(i, c=c):
                means[pl.ds(2 * i, 2), :] = one(i, c)
                return i + 1

            lo = lax.while_loop(lambda i: i <= hi - step, body, lo)
            lax.while_loop(lambda i: i < hi, rest, lo)
        return carry

    lax.fori_loop(0, QUARTERS, quarter, 0)

    def own(t, carry):
        i = t * MOVES
        move = [moves[i + u] for u in range(MOVES)]
        for u in range(MOVES):
            selfs[pl.ds(2 * i + 2 * u, 2), :] = load(move[u] & 65535)
            mean = pl.multiple_of(lax.shift_right_logical(move[u], 16), 2)
            sums[pl.ds(2 * i + 2 * u, 2), :] = means[pl.ds(mean, 2), :]
        return carry

    lax.fori_loop(0, 2 * npair // MOVES, own, 0)

    rows = ROWS

    def dense(t, carry):
        embs = []
        for side in range(2):
            r0 = (side * npair + t * rows) * 2
            x = jnp.concatenate(
                [
                    ref[pl.ds(r0 + h, rows, 2), :].astype(jnp.bfloat16)
                    for ref in (selfs, sums)
                    for h in range(2)
                ],
                axis=1,
            )
            pre = jnp.dot(x, mats[:512], preferred_element_type=jnp.float32) + vecs[0:1]
            act = jnp.maximum(pre, 0.0)
            ms = jnp.mean(act * act, axis=-1, keepdims=True)
            embs.append((act * lax.rsqrt(ms + 1e-6)).astype(jnp.bfloat16).astype(jnp.float32))
        had = (embs[0] * embs[1]).astype(jnp.bfloat16)
        first = jnp.dot(had, mats[512:768], preferred_element_type=jnp.float32) + vecs[1:2]
        first = jnp.maximum(first, 0.0).astype(jnp.bfloat16)
        second = jnp.dot(first, mats[768:], preferred_element_type=jnp.float32) + vecs[2:3]
        second = jnp.maximum(second, 0.0) * vecs[3:4]
        logit = lax.dot_general(
            jnp.ones((8, 128), jnp.float32),
            second[:, :128] + second[:, 128:],
            (((1,), (1,)), ((), ())),
            precision=lax.Precision.HIGHEST,
            preferred_element_type=jnp.float32,
        )[:1]
        k = t * rows + lax.broadcasted_iota(jnp.int32, (1, rows), 1)
        x = jnp.where(k < npair // 4, -logit, logit)
        x = jnp.maximum(x, 0.0) + jnp.log1p(jnp.exp(-jnp.abs(x)))
        for u in range(rows // 128):
            out[pl.ds(t * (rows // 128) + u, 1), :] = x[:, u * 128 : (u + 1) * 128]
        return carry

    lax.fori_loop(0, npair // rows, dense, 0)


def score(starts, spots, moves, ids, table, mats, vecs, npair):
    nodes = table.shape[0]
    return pl.pallas_call(
        functools.partial(score_kernel, npair=npair),
        out_shape=jax.ShapeDtypeStruct((npair // 128, 128), jnp.float32),
        in_specs=[SMEM] + [ANY] * 4 + [VMEM] * 2,
        out_specs=VMEM,
        scratch_shapes=[
            pltpu.VMEM((nodes, 2, 128), jnp.bfloat16),
            pltpu.VMEM((4 * npair, 128), jnp.float32),
            pltpu.VMEM((4 * npair, 128), jnp.float32),
            pltpu.VMEM((4 * npair, 128), jnp.float32),
            pltpu.SemaphoreType.DMA,
            pltpu.SemaphoreType.DMA((2, WORDS)),
            pltpu.SemaphoreType.DMA((2,)),
            pltpu.SMEM((2 * npair,), jnp.int32),
            pltpu.SMEM((2 * npair,), jnp.int32),
        ]
        + [pltpu.SMEM((2 * ids.shape[0] // (QUARTERS * WORDS),), jnp.int32)] * WORDS,
        compiler_params=pltpu.CompilerParams(vmem_limit_bytes=56 * 2**20),
    )(starts, spots, moves, ids, table, mats, vecs)


def on_device(
    features, neighbors, counts, pairs, w_self, w_neigh, b_layer, w_one, b_one, w_two, b_two, w_out
):
    span, cols = features.shape
    parts, shards = lax.axis_size("pair"), lax.axis_size("node")
    npair = pairs.shape[0]
    slab = lax.all_to_all(
        features.reshape(parts, span // parts, cols), "pair", split_axis=0, concat_axis=0, tiled=True
    )
    slab = slab.transpose(1, 0, 2).reshape(span // parts, 2, parts * cols // 2)
    table = lax.all_gather(slab, ("node", "pair"), axis=0, tiled=True)
    ids = neighbors[0].T
    info = jnp.concatenate([ids[0::2] | (ids[1::2] << 16), counts], axis=0)
    info = lax.all_gather(info, "node", axis=0)
    share = span * shards // QUARTERS
    ids = info[:, :WORDS].reshape(QUARTERS, -1, WORDS, span).transpose(0, 2, 1, 3).reshape(-1)
    ends = pairs.T.reshape(-1)
    code = ends // share * FAN + look_up(ends, info[:, WORDS].reshape(-1)) - 1
    keys = ((code - 32) << 26) | ((ends & (share - 1)) << 13) | jnp.arange(2 * npair, dtype=jnp.int32)
    keys = lax.sort(keys)
    node = keys >> 13
    new = jnp.concatenate([jnp.ones((1,), jnp.int32), (node[1:] != node[:-1]).astype(jnp.int32)])
    rank = jnp.cumsum(new) - 1
    place = lax.sort(((keys & 8191) << 13) | rank) & 8191
    moves = ends | (place << 17)
    code = (keys >> 26) + 32
    marks = jnp.arange(QUARTERS * FAN + 1, dtype=jnp.int32)
    starts = jnp.sum((code[None, :] < marks[:, None]).astype(jnp.int32) * new[None, :], axis=1)
    spots = (node & (share - 1)) + (code // FAN & 1) * share
    order = jnp.arange(2 * npair, dtype=jnp.int32) << 14
    spots = lax.sort(spots | order | ((1 - new) << 28)) & 16383
    mats = jnp.concatenate([w_self, w_neigh, w_one, w_two], axis=0)
    vecs = jnp.stack([b_layer, b_one, b_two, w_out])
    loss = score(starts, spots, moves, ids, table, mats, vecs, npair)
    return loss.reshape(-1)


def solution(mesh):
    in_specs = (
        P("node", "pair"),
        P("pair", "node", None),
        P("pair", "node"),
        P(("pair", "node"), None),
    ) + (P(),) * 8
    return jax.shard_map(
        on_device, mesh=mesh, in_specs=in_specs, out_specs=P(("pair", "node")), check_vma=False
    )
```

```python
import functools
import jax
import jax.numpy as jnp
from jax import lax
from jax.experimental import pallas as pl
from jax.experimental.pallas import tpu as pltpu
from jax.sharding import PartitionSpec as P

QUARTERS = 4
FAN = 10
WORDS = FAN // 2
STEP = 16
MOVES = 128
ROWS = 1024
STEPS = (16, 16, 16, 16, 16, 16, 16, 16, 16, 16)
SMEM = pl.BlockSpec(memory_space=pltpu.SMEM)
VMEM = pl.BlockSpec(memory_space=pltpu.VMEM)
ANY = pl.BlockSpec(memory_space=pl.ANY)


def look_up_kernel(where, values, out, *, step):
    def body(t, carry):
        for u in range(step):
            out[t * step + u] = values[where[t * step + u]]
        return carry

    lax.fori_loop(0, where.shape[0] // step, body, 0)


def look_up(where, values):
    return pl.pallas_call(
        functools.partial(look_up_kernel, step=STEP),
        out_shape=jax.ShapeDtypeStruct(where.shape, jnp.int32),
        in_specs=[SMEM] * 2,
        out_specs=SMEM,
        cost_estimate=pl.CostEstimate(flops=0, bytes_accessed=2**25, transcendentals=0),
    )(where, values)


def score_kernel(*refs, npair):
    starts, spots_hbm, moves_hbm, ids_hbm = refs[:4]
    table, mats, vecs, out, tab, means, sums, selfs, tab_sem, ids_sem, list_sem, spots, moves = refs[4:17]
    ids = refs[17:]
    part = ids_hbm.shape[0] // (QUARTERS * WORDS)

    def fetch(q):
        slot = q & 1
        return [
            pltpu.make_async_copy(
                ids_hbm.at[pl.ds((q * WORDS + j) * part, part)],
                ids[j].at[pl.ds(slot * part, part)],
                ids_sem.at[slot, j],
            )
            for j in range(WORDS)
        ]

    for copy in fetch(0):
        copy.start()
    lists = [
        pltpu.make_async_copy(spots_hbm, spots, list_sem.at[0]),
        pltpu.make_async_copy(moves_hbm, moves, list_sem.at[1]),
    ]
    for copy in lists:
        copy.start()
    pltpu.make_async_copy(table, tab, tab_sem).start()
    pltpu.make_async_copy(table, tab, tab_sem).wait()
    for copy in lists:
        copy.wait()

    def load(n):
        return tab[n].astype(jnp.float32)

    def one(i, c):
        spot = spots[i]
        words = [ids[j][spot] for j in range((c + 1) // 2)]
        rows = [
            load(lax.shift_right_logical(words[j // 2], 16) if j % 2 else words[j // 2] & 65535)
            for j in range(c)
        ]
        while len(rows) > 1:
            rows = [sum(rows[k + 1 : k + 2], rows[k]) for k in range(0, len(rows), 2)]
        return rows[0] if c == 1 else rows[0] * jnp.float32(1.0 / c)

    def quarter(q, carry):
        for copy in fetch(q):
            copy.wait()

        @pl.when(q < QUARTERS - 1)
        def _():
            for copy in fetch(q + 1):
                copy.start()

        for c in range(1, FAN + 1):
            lo = starts[q * FAN + c - 1]
            hi = starts[q * FAN + c]
            step = STEPS[c - 1]

            def body(i, c=c, step=step):
                got = [one(i + u, c) for u in range(step)]
                for u in range(step):
                    means[pl.ds(2 * i + 2 * u, 2), :] = got[u]
                return i + step

            lo = lax.while_loop(lambda i: i <= hi - step, body, lo)
            lo = lax.while_loop(lambda i: i <= hi - 3, functools.partial(body, step=3), lo)
            lax.while_loop(lambda i: i < hi, functools.partial(body, step=1), lo)
        return carry

    lax.fori_loop(0, QUARTERS, quarter, 0)

    def own(t, carry):
        i = t * MOVES
        move = [moves[i + u] for u in range(MOVES)]
        for u in range(MOVES):
            selfs[pl.ds(2 * i + 2 * u, 2), :] = load(move[u] & 65535)
            mean = pl.multiple_of(lax.shift_right_logical(move[u], 16), 2)
            sums[pl.ds(2 * i + 2 * u, 2), :] = means[pl.ds(mean, 2), :]
        return carry

    lax.fori_loop(0, 2 * npair // MOVES, own, 0)

    rows = ROWS

    def dense(t, carry):
        embs = []
        for side in range(2):
            r0 = (side * npair + t * rows) * 2
            x = jnp.concatenate(
                [
                    ref[pl.ds(r0 + h, rows, 2), :].astype(jnp.bfloat16)
                    for ref in (selfs, sums)
                    for h in range(2)
                ],
                axis=1,
            )
            pre = jnp.dot(x, mats[:512], preferred_element_type=jnp.float32) + vecs[0:1]
            act = jnp.maximum(pre, 0.0)
            ms = jnp.mean(act * act, axis=-1, keepdims=True)
            embs.append((act * lax.rsqrt(ms + 1e-6)).astype(jnp.bfloat16).astype(jnp.float32))
        had = (embs[0] * embs[1]).astype(jnp.bfloat16)
        first = jnp.dot(had, mats[512:768], preferred_element_type=jnp.float32) + vecs[1:2]
        first = jnp.maximum(first, 0.0).astype(jnp.bfloat16)
        second = jnp.dot(first, mats[768:], preferred_element_type=jnp.float32) + vecs[2:3]
        second = jnp.maximum(second, 0.0) * vecs[3:4]
        logit = lax.dot_general(
            jnp.ones((8, 128), jnp.float32),
            second[:, :128] + second[:, 128:],
            (((1,), (1,)), ((), ())),
            precision=lax.Precision.HIGHEST,
            preferred_element_type=jnp.float32,
        )[:1]
        k = t * rows + lax.broadcasted_iota(jnp.int32, (1, rows), 1)
        x = jnp.where(k < npair // 4, -logit, logit)
        x = jnp.maximum(x, 0.0) + jnp.log1p(jnp.exp(-jnp.abs(x)))
        for u in range(rows // 128):
            out[pl.ds(t * (rows // 128) + u, 1), :] = x[:, u * 128 : (u + 1) * 128]
        return carry

    lax.fori_loop(0, npair // rows, dense, 0)


def score(starts, spots, moves, ids, table, mats, vecs, npair):
    nodes = table.shape[0]
    return pl.pallas_call(
        functools.partial(score_kernel, npair=npair),
        out_shape=jax.ShapeDtypeStruct((npair // 128, 128), jnp.float32),
        in_specs=[SMEM] + [ANY] * 4 + [VMEM] * 2,
        out_specs=VMEM,
        scratch_shapes=[
            pltpu.VMEM((nodes, 2, 128), jnp.bfloat16),
            pltpu.VMEM((4 * npair, 128), jnp.float32),
            pltpu.VMEM((4 * npair, 128), jnp.float32),
            pltpu.VMEM((4 * npair, 128), jnp.float32),
            pltpu.SemaphoreType.DMA,
            pltpu.SemaphoreType.DMA((2, WORDS)),
            pltpu.SemaphoreType.DMA((2,)),
            pltpu.SMEM((2 * npair,), jnp.int32),
            pltpu.SMEM((2 * npair,), jnp.int32),
        ]
        + [pltpu.SMEM((2 * ids.shape[0] // (QUARTERS * WORDS),), jnp.int32)] * WORDS,
        compiler_params=pltpu.CompilerParams(vmem_limit_bytes=56 * 2**20),
    )(starts, spots, moves, ids, table, mats, vecs)


def on_device(
    features, neighbors, counts, pairs, w_self, w_neigh, b_layer, w_one, b_one, w_two, b_two, w_out
):
    span, cols = features.shape
    parts, shards = lax.axis_size("pair"), lax.axis_size("node")
    npair = pairs.shape[0]
    slab = lax.all_to_all(
        features.reshape(parts, span // parts, cols), "pair", split_axis=0, concat_axis=0, tiled=True
    )
    slab = slab.transpose(1, 0, 2).reshape(span // parts, 2, parts * cols // 2)
    table = lax.all_gather(slab, ("node", "pair"), axis=0, tiled=True)
    ids = neighbors[0].T
    info = jnp.concatenate([ids[0::2] | (ids[1::2] << 16), counts], axis=0)
    info = lax.all_gather(info, "node", axis=0)
    share = span * shards // QUARTERS
    ids = info[:, :WORDS].reshape(QUARTERS, -1, WORDS, span).transpose(0, 2, 1, 3).reshape(-1)
    ends = pairs.T.reshape(-1)
    code = ends // share * FAN + look_up(ends, info[:, WORDS].reshape(-1)) - 1
    keys = ((code - 32) << 26) | ((ends & (share - 1)) << 13) | jnp.arange(2 * npair, dtype=jnp.int32)
    keys = lax.sort(keys)
    node = keys >> 13
    new = jnp.concatenate([jnp.ones((1,), jnp.int32), (node[1:] != node[:-1]).astype(jnp.int32)])
    rank = jnp.cumsum(new) - 1
    place = lax.sort(((keys & 8191) << 13) | rank) & 8191
    moves = ends | (place << 17)
    code = (keys >> 26) + 32
    marks = jnp.arange(QUARTERS * FAN + 1, dtype=jnp.int32)
    starts = jnp.sum((code[None, :] < marks[:, None]).astype(jnp.int32) * new[None, :], axis=1)
    spots = (node & (share - 1)) + (code // FAN & 1) * share
    order = jnp.arange(2 * npair, dtype=jnp.int32) << 14
    spots = lax.sort(spots | order | ((1 - new) << 28)) & 16383
    mats = jnp.concatenate([w_self, w_neigh, w_one, w_two], axis=0)
    vecs = jnp.stack([b_layer, b_one, b_two, w_out])
    loss = score(starts, spots, moves, ids, table, mats, vecs, npair)
    return loss.reshape(-1)


def solution(mesh):
    in_specs = (
        P("node", "pair"),
        P("pair", "node", None),
        P("pair", "node"),
        P(("pair", "node"), None),
    ) + (P(),) * 8
    return jax.shard_map(
        on_device, mesh=mesh, in_specs=in_specs, out_specs=P(("pair", "node")), check_vma=False
    )
```
